512 devices in a mesh: seq: 16 (over y, core), dp: 32 (over z, x).
Axes of the slice: x: 4, y: 8, z: 8, core: 2. Of those that a mesh axis runs over, the one named last changes fastest.
Arguments:
- latents: bfloat16 [64, 48, 128, 1152], P('dp', 'seq'), parts along dimension 0, may hold values from -6 to 6
- modulation: float32 [64, 3, 1152], P('dp'), parts along dimension 0, may hold values from -4 to 4
- w_qkv: bfloat16 [1152, 1728], P(None, 'seq'), may hold values from -0.1875 to 0.1875
- w_out: bfloat16 [576, 1152], P('seq'), may hold values from -0.25 to 0.25
- clip_frames: int32 [64], P('dp'), parts along dimension 0, may hold values from 12 to 48, as said below
- time_positions: int32 [64, 48], P('dp'), parts along dimension 0, may hold values from 0 to 204, as said below
Outputs:
- updated: bfloat16 [64, 48, 128, 1152], P('dp', 'seq'), parts along dimension 0
The draws below stay inside these ranges and needn't reach their ends.
There are 32 independent parts, one for each index of `dp`. The reference program is written for one: setup_inputs(seed, part) draws one part's arguments, and reference() takes and returns one part's arrays. A program takes and returns all parts, laid end to end along the dimension named above; an argument that names none is the same for every part. Nothing has to cross between parts.
Inputs may be any that keep to these rules, and one draw needn't show every extreme that they name: Frames 0 to clip_frames - 1 of a clip hold data; at least 12 of them; some clip of every group has all 48. `time_positions`: within a clip the positions rise by 1 to 3 from each frame slot to the next; in every group some clip starts at 0 and some clip ends at 204.
All inputs are finite; a program needn't handle non-finite values.
Results may differ from the reference program's by a relative error of at most 0.0035.
Values may be sent and summed in bfloat16 or wider, within the bound.
A program may use at most 64 MiB of HBM per device.

```python
import math
import jax
import jax.numpy as jnp
from jax import lax

D = 1152
H = 8
HD = 72
CLIPS = 2
PATCH = 128
FRAMES = 48


def draw_clip_frames(key, part):
    key = jax.random.fold_in(key, 11)
    first, second = jax.random.split(key)
    lowest = max(1, FRAMES // 4)
    counts = jax.random.randint(first, (CLIPS,), lowest, FRAMES + 1)
    chosen = jax.random.randint(second, (), 0, CLIPS)
    return counts.at[chosen].set(FRAMES).astype(jnp.int32)


def draw_time_positions(key, part):
    key = jax.random.fold_in(key, 23)
    first, second = jax.random.split(key)
    increments = jax.random.randint(first, (CLIPS, FRAMES), 1, 4).astype(jnp.int32)
    increments = increments.at[:, 0].set(0)
    rising = jnp.cumsum(increments, axis=1).astype(jnp.int32)
    top = 63 + 3 * (FRAMES - 1)
    chosen = jax.random.randint(second, (), 0, CLIPS)
    other = (chosen + 1) % CLIPS
    offset = jnp.zeros((CLIPS,), jnp.int32)
    offset = offset.at[other].set(top - rising[other, FRAMES - 1])
    offset = offset.at[chosen].set(0)
    return (offset[:, None] + rising).astype(jnp.int32)


def block_scale(own_key, dims, shards, low, high):
    loudness, own = 1.0, jax.random.fold_in(own_key, 6)
    for axis_at, blocks in shards:
        draws = jnp.exp(jax.random.uniform(jax.random.fold_in(own, axis_at), (blocks,), jnp.float32, low / len(shards), high / len(shards)))
        loudness = loudness * jnp.repeat(draws, dims[axis_at] // blocks).reshape([-1 if axis == axis_at else 1 for axis in range(len(dims))])
    return loudness


def normal_values(key, dims, spread, limit, pieces=(), kind=jnp.bfloat16):
    drawn = jax.random.normal(key, dims, jnp.float32) * spread
    if len(pieces) > 0:
        drawn = block_scale(key, dims, pieces, -0.22, 0.18) * drawn
    return jnp.clip(drawn, min=-limit, max=limit).astype(kind)


def setup_inputs(seed: int = 0, part: int = 0) -> dict:
    streams_of = jax.random.split(jax.random.key(seed), 7)
    part_keys = jax.random.split(jax.random.fold_in(streams_of[6], part), 7)
    return {
        "latents": normal_values(part_keys[0], (CLIPS, FRAMES, PATCH, D), 1.0, 6.0, ((1, 16),)),
        "modulation": normal_values(part_keys[1], (CLIPS, 3, D), 0.7, 4.0, (), jnp.float32),
        "w_qkv": normal_values(streams_of[2], (D, 3 * H * HD), D ** -0.5, 0.1875, ((1, 16),)),
        "w_out": normal_values(streams_of[3], (H * HD, D), (H * HD) ** -0.5, 0.25, ((0, 16),)),
        "clip_frames": draw_clip_frames(jax.random.fold_in(jax.random.fold_in(streams_of[6], part), 71), part),
        "time_positions": draw_time_positions(jax.random.fold_in(jax.random.fold_in(streams_of[6], part), 71), part),
    }


def modulate(latents, modulation):
    values = latents.astype(jnp.float32)
    mean = lax.optimization_barrier(jnp.mean(values, axis=-1, keepdims=True))
    var = lax.optimization_barrier(jnp.mean((values - mean) ** 2, axis=-1, keepdims=True))
    normed = (values - mean) * lax.rsqrt(var + 1e-06)
    shift = modulation[:, 0][:, None, None, :]
    scale = modulation[:, 1][:, None, None, :]
    return (normed * (1.0 + scale) + shift).astype(jnp.bfloat16)

def rms_norm(vec):
    return vec * lax.rsqrt(lax.optimization_barrier(jnp.mean(vec * vec, axis=-1, keepdims=True)) + 1e-06)

def rotate(vec, angle):
    pairs = vec.reshape(vec.shape[:-1] + (HD // 2, 2))
    first = pairs[..., 0]
    second = pairs[..., 1]
    cosine = jnp.cos(angle)
    sine = jnp.sin(angle)
    turned = jnp.stack([first * cosine - second * sine, first * sine + second * cosine], axis=-1)
    return turned.reshape(vec.shape)

def attend(qkv, clip_frames, time_positions):
    clips, frames, patches, width = qkv.shape
    parts = qkv.reshape(clips, frames, patches, 3, H, HD)
    index = jnp.arange(HD // 2).astype(jnp.float32)
    freq = jnp.exp(-math.log(10000.0) * 2.0 * index / HD)
    angle = time_positions.astype(jnp.float32)[:, :, None, None, None] * freq
    query = rotate(rms_norm(parts[:, :, :, 0].astype(jnp.float32)), angle).astype(jnp.bfloat16)
    keys = rotate(rms_norm(parts[:, :, :, 1].astype(jnp.float32)), angle).astype(jnp.bfloat16)
    values = parts[:, :, :, 2]
    scores = jnp.einsum('btphd,bsphd->bphts', query.astype(jnp.float32), keys.astype(jnp.float32))
    scores = scores * (1.0 / math.sqrt(HD))
    live = jnp.arange(frames).astype(jnp.int32)[None, :] < clip_frames[:, None]
    expo = jnp.where(live[:, None, None, None, :], jnp.exp(scores), 0.0)
    weights = (expo / lax.optimization_barrier(jnp.sum(expo, axis=-1, keepdims=True))).astype(jnp.bfloat16)
    attended = jnp.einsum('bphts,bsphd->btphd', weights.astype(jnp.float32), values.astype(jnp.float32))
    return attended.astype(jnp.bfloat16).reshape(clips, frames, patches, H * HD)

def reference(latents, modulation, w_qkv, w_out, clip_frames, time_positions):
    clips, frames, patches, width = latents.shape
    modulated = modulate(latents, modulation)
    qkv = jnp.dot(modulated.reshape(-1, width), w_qkv, preferred_element_type=jnp.float32).astype(jnp.bfloat16)
    attended = attend(qkv.reshape(clips, frames, patches, -1), clip_frames, time_positions)
    projected = jnp.dot(attended.reshape(-1, H * HD), w_out, preferred_element_type=jnp.float32)
    live = (jnp.arange(frames).astype(jnp.int32)[None, :] < clip_frames[:, None]).astype(jnp.float32)
    gate = modulation[:, 2][:, None, None, :]
    result = latents.astype(jnp.float32) + live[:, :, None, None] * gate * projected.reshape(clips, frames, patches, width)
    return result.astype(jnp.bfloat16)
```

```python
import functools
import math

import jax
import jax.numpy as jnp
from jax import lax
from jax.experimental import pallas as pl
from jax.experimental.pallas import tpu as pltpu
from jax.sharding import PartitionSpec as P

MESH = pl.DeviceIdType.MESH
F32 = jnp.float32
BF16 = jnp.bfloat16

D = 1152
H = 8
HD = 72
C = 2
T = 48
SEQ = 16
NX = 4
NZ = 8
NY = 8
TL = 3
PL = 8
TOK = T * PL
HP = 80
QK = H * HP
KT = D // 128
ZREL = (0, 1, 7, 2, 6, 3, 5, 4)


def nt(a, b):
    return lax.dot_general(a, b, (((1,), (1,)), ((), ())), preferred_element_type=F32)


def nn(a, b):
    return lax.dot_general(a, b, (((1,), (0,)), ((), ())), preferred_element_type=F32)


def row_ids(shape):
    return lax.broadcasted_iota(jnp.int32, shape, 0)


def lane_ids(shape):
    return lax.broadcasted_iota(jnp.int32, shape, 1)


def normalise(xin, xm, mod_ref, c):
    @pl.loop(0, SEQ // 2)
    def _(k):
        v = xin[c, pl.ds(2 * k, 2)].astype(F32).reshape(2 * TL * PL, D)
        mean = jnp.mean(v, axis=-1, keepdims=True)
        v = v - mean
        var = jnp.mean(v * v, axis=-1, keepdims=True)
        normed = v * lax.rsqrt(var + 1e-6)
        shift = mod_ref[c, 0:1, :]
        scale = mod_ref[c, 1:2, :]
        rows = pl.ds(pl.multiple_of(48 * k, 48), 48)
        xm[c, rows, :] = (normed * (1.0 + scale) + shift).astype(BF16)


def tables(tp_ref, cf_ref, cos_t, even_t, odd_t, mask_t):
    shape = (HP, TOK)
    r = row_ids(shape)
    within = jnp.where(r >= 40, r - 40, r)
    feature = jnp.where(r >= 40, within + 36, within)
    pair = lax.shift_right_logical(feature, 1)
    freq = jnp.exp(pair.astype(F32) * (-math.log(10000.0) * 2.0 / HD))
    is_even = (r & 1) == 0
    frame = lax.shift_right_logical(lane_ids((8, TOK)), 3)
    key = row_ids((TOK, TOK))
    query = lane_ids((TOK, TOK))
    same = (key & 7) == (query & 7)
    key_frame = lax.shift_right_logical(key, 3)
    for c in range(C):
        pos = jnp.zeros((8, TOK), F32)
        for t in range(T):
            pos = jnp.where(frame == t, tp_ref[c, t].astype(F32), pos)
        angle = freq * pos[0:1]
        sine = jnp.sin(angle)
        cos_t[c] = jnp.cos(angle)
        even_t[c] = jnp.where(is_even, -sine, 0.0)
        odd_t[c] = jnp.where(is_even, 0.0, sine)
        live = same & (key_frame < cf_ref[c])
        mask_t[c] = jnp.where(live, 1.0, 0.0).astype(BF16)


def pack_weights(wq_ref, wo_ref, wloc):
    for i in range(64):
        d, j = divmod(i, 2)
        kt, rt = divmod(i, 7)
        if kt < KT and rt < 6:
            tile = wq_ref[16 * rt : 16 * rt + 16, 128 * kt : 128 * kt + 128]
        elif kt < KT:
            part = wq_ref[96:108, 128 * kt : 128 * kt + 128].astype(F32)
            tile = jnp.concatenate([part, jnp.zeros((4, 128), F32)], axis=0).astype(BF16)
        else:
            tile = jnp.zeros((16, 128), BF16)
        wloc[d // NZ, d % NZ, j] = tile
    for d in range(32):
        kt, rt = divmod(d, 3)
        if kt < KT and rt < 2:
            tile = wo_ref[16 * rt : 16 * rt + 16, 128 * kt : 128 * kt + 128]
        elif kt < KT:
            part = wo_ref[32:36, 128 * kt : 128 * kt + 128].astype(F32)
            tile = jnp.concatenate([part, jnp.zeros((12, 128), F32)], axis=0).astype(BF16)
        else:
            tile = jnp.zeros((16, 128), BF16)
        wloc[d // NZ, d % NZ, 2] = tile


def spread_rows(g, y, kt, core):
    tiles = []
    for i in range(7 * kt, 7 * kt + 7):
        d, j = divmod(i, 2)
        tiles.append(g[core, y, d // NZ, d % NZ, j].astype(F32))
    w = jnp.concatenate(tiles, axis=0)
    moved = pltpu.roll(w, 4, 0)
    r = row_ids((40, 128))
    first = jnp.where(r < 36, w[0:40], 0.0)
    second = jnp.where(r < 36, moved[40:80], 0.0)
    return [first, second, w[72:112]]


def unpack_qkv(g, wt):
    @pl.loop(0, NY)
    def _(y):
        for kt in range(KT):
            rows = spread_rows(g, y, kt, 0) + spread_rows(g, y, kt, 1)
            block = jnp.concatenate(rows, axis=0).astype(BF16)
            wt[pl.ds(pl.multiple_of(240 * y, 240), 240), 128 * kt : 128 * kt + 128] = block


def unpack_out(g, wot):
    @pl.loop(0, NY)
    def _(y):
        for kt in range(KT):
            rows = []
            for core in range(2):
                tiles = []
                for d in range(3 * kt, 3 * kt + 3):
                    tiles.append(g[core, y, d // NZ, d % NZ, 2].astype(F32))
                rows.append(jnp.concatenate(tiles, axis=0)[0:40])
            block = jnp.concatenate(rows, axis=0).astype(BF16)
            wot[pl.ds(pl.multiple_of(HP * y, HP), HP), 128 * kt : 128 * kt + 128] = block


def rotate(v, cos, even, odd):
    total = jnp.sum(v * v, axis=0, keepdims=True)
    v = v * lax.rsqrt(total * (1.0 / HD) + 1e-6)
    up = pltpu.roll(v, HP - 1, 0)
    down = pltpu.roll(v, 1, 0)
    return (v * cos + up * even + down * odd).astype(BF16)


def attend(c, xm, wt, qkv_t, att_t, back, cos_t, even_t, odd_t, mask_t):
    x = xm[c]
    for block in range(3):
        rows = slice(QK * block, QK * (block + 1))
        qkv_t[rows, :] = nt(wt[rows, :], x).astype(BF16)

    ones_row = jnp.where(row_ids((HP, 1)) == 36, 1.0, 0.0).astype(BF16)

    for h in range(H):
        rows = HP * h
        cos, even, odd = cos_t[c], even_t[c], odd_t[c]
        q = rotate(qkv_t[rows : rows + HP].astype(F32), cos, even, odd)
        k = rotate(qkv_t[QK + rows : QK + rows + HP].astype(F32), cos, even, odd)
        v = qkv_t[2 * QK + rows : 2 * QK + rows + HP] + ones_row
        s = nn(k.T, q)
        e = jnp.exp(s * (1.0 / math.sqrt(HD))).astype(BF16) * mask_t[c]
        o = nn(v, e)
        att_t[rows : rows + HP] = (o / o[36:37]).astype(BF16)
    for j in range(QK // 128):
        lanes = slice(128 * j, 128 * j + 128)
        part = att_t[lanes, :].astype(F32).T
        back[c, :, :, :, lanes] = part.reshape(SEQ, TL, PL, 128).astype(BF16)


def kernel(
    lat, mod_ref, wq_ref, wo_ref, cf_ref, tp_ref, out,
    xin, xm, wloc, g, wt, wot, qkv_t, att_t, back, got, held, outv, cos_t, even_t, odd_t, mask_t,
    a_s, a_r, z_s, z_r, x_s, x_r, cq_s, cq_r, co_s, co_r, f_s, f_r, r_s, r_r, own_sem, held_sem, out_sem,
):
    s_me = lax.axis_index("seq")
    d_me = lax.axis_index("dp")
    y, core = s_me // 2, s_me % 2
    z, x = d_me // NX, d_me % NX

    def seq_id(s):
        return (s, d_me)

    def plane_id(zz, xx):
        return (s_me, zz * NX + xx)

    right = plane_id(z, (x + 1) % NX)
    left = plane_id(z, (x + NX - 1) % NX)
    sibling = seq_id(s_me + 1 - 2 * core)

    def remote(src, dst, send, recv, to):
        return pltpu.make_async_remote_copy(
            src_ref=src, dst_ref=dst, send_sem=send, recv_sem=recv, device_id=to, device_id_type=MESH
        )

    barrier = pltpu.get_barrier_semaphore()
    for r in range(1, SEQ):
        pl.semaphore_signal(barrier, inc=1, device_id=seq_id((s_me + r) % SEQ), device_id_type=MESH)
    for r in range(1, NZ):
        pl.semaphore_signal(barrier, inc=1, device_id=plane_id((z + r) % NZ, x), device_id_type=MESH)
    pl.semaphore_signal(barrier, inc=1, device_id=right, device_id_type=MESH)
    pl.semaphore_signal(barrier, inc=1, device_id=left, device_id_type=MESH)

    own = [pltpu.make_async_copy(lat.at[c, :, s_me], xin.at[c, s_me], own_sem.at[c]) for c in range(C)]
    for c in range(C):
        own[c].start()
    hold = pltpu.make_async_copy(lat, held, held_sem)
    hold.start()
    pack_weights(wq_ref, wo_ref, wloc)
    g[core, y, x, z] = wloc[x, z]
    pl.semaphore_wait(barrier, SEQ - 1 + NZ - 1 + 2)

    def piece(r):
        yy = (y + r) % NY
        return remote(wloc.at[x, z], g.at[core, y, x, z], a_s.at[r], a_r.at[r], seq_id(2 * yy + core))

    for r in (1, 7, 2, 6, 3, 5, 4):
        piece(r).start()

    def forth(c, r):
        to = (s_me + r) % SEQ
        return remote(lat.at[c, :, to], xin.at[c, s_me], f_s.at[c, r], f_r.at[c, r], seq_id(to))

    for r in (1, 15, 2, 14, 3, 13, 4, 12, 5, 11, 6, 10, 7, 9, 8):
        forth(0, r).start()

    tiles = (slice(0, 2), slice(2, 3))

    def part(kind, core_of, xx, zz):
        return g.at[core_of, :, xx, zz, tiles[kind]]

    def z_copy(kind, r):
        to = plane_id((z + r) % NZ, x)
        mine = part(kind, core, x, z)
        return remote(mine, mine, z_s.at[kind, r], z_r.at[kind, r], to)

    def x_copy(kind, way, k, xx, zz, to):
        block = part(kind, core, xx, zz)
        return remote(block, block, x_s.at[kind, way, k], x_r.at[kind, way, k], to)

    def core_copy_q(xr, k):
        block = part(0, core, (x + xr) % NX, (z + ZREL[k]) % NZ)
        return remote(block, block, cq_s.at[xr, k], cq_r.at[xr, k], sibling)

    def core_copy_o(xr):
        block = g.at[core, :, (x + xr) % NX, :, tiles[1]]
        return remote(block, block, co_s.at[xr], co_r.at[xr], sibling)

    for r in (1, 7, 2, 6, 3, 5, 4):
        piece(r).wait_recv()
    for r in (1, 7, 2, 6, 3, 5, 4):
        z_copy(0, r).start()
    for r in (1, 15, 2, 14, 3, 13, 4, 12, 5, 11, 6, 10, 7, 9, 8):
        forth(1, r).start()
    for r in (1, 7, 2, 6, 3, 5, 4):
        z_copy(1, r).start()

    tables(tp_ref, cf_ref, cos_t, even_t, odd_t, mask_t)

    def from_z(kind):
        for k, rel in enumerate(ZREL):
            zz = (z + rel) % NZ
            if rel:
                z_copy(kind, (NZ - rel) % NZ).wait_recv()
            x_copy(kind, 0, k, x, zz, right).start()
            x_copy(kind, 1, k, x, zz, left).start()
            if kind == 0:
                core_copy_q(0, k).start()

    def from_x(kind):
        before, after, across = (x + NX - 1) % NX, (x + 1) % NX, (x + 2) % NX

        def crossed(k):
            zz = (z + ZREL[k]) % NZ
            x_copy(kind, 2, k, across, zz, right).wait_recv()
            if kind == 0:
                core_copy_q(2, k).start()

        for k, rel in enumerate(ZREL):
            zz = (z + rel) % NZ

            def first():
                x_copy(kind, 0, k, before, zz, right).wait_recv()
                if k % 2 == 0:
                    x_copy(kind, 2, k, before, zz, right).start()
                if kind == 0:
                    core_copy_q(3, k).start()

            def second():
                x_copy(kind, 1, k, after, zz, left).wait_recv()
                if k % 2 == 1:
                    x_copy(kind, 2, k, after, zz, left).start()
                if kind == 0:
                    core_copy_q(1, k).start()

            if k % 2 == 0:
                first()
                second()
            else:
                second()
                first()
            if k >= 2:
                crossed(k - 2)
        crossed(6)
        crossed(7)

    from_z(0)
    from_z(1)
    from_x(0)

    def arrived(c):
        own[c].wait()
        for r in range(1, SEQ):
            forth(c, r).wait_recv()

    def give_back(c, r):
        to = (s_me + r) % SEQ
        return remote(back.at[c, to], got.at[c, :, s_me], r_s.at[c, r], r_r.at[c, r], seq_id(to))

    def keep(c):
        return pltpu.make_async_copy(back.at[c, s_me], got.at[c, :, s_me], own_sem.at[c])

    def clip(c):
        attend(c, xm, wt, qkv_t, att_t, back, cos_t, even_t, odd_t, mask_t)
        keep(c).start()
        for r in (1, 15, 2, 14, 3, 13, 4, 12, 5, 11, 6, 10, 7, 9, 8):
            give_back(c, r).start()

    arrived(0)
    normalise(xin, xm, mod_ref, 0)
    for k in range(NZ):
        for xr in range(NX):
            core_copy_q(xr, k).wait_recv()
    unpack_qkv(g, wt)
    clip(0)

    from_x(1)
    for xr in range(NX):
        core_copy_o(xr).start()
    arrived(1)
    normalise(xin, xm, mod_ref, 1)
    clip(1)
    for xr in range(NX):
        core_copy_o(xr).wait_recv()
    unpack_out(g, wot)
    hold.wait()

    def out_copy(c, f):
        return pltpu.make_async_copy(outv.at[c, f], out.at[c, f], out_sem.at[c, f])

    for c in range(C):
        keep(c).wait()
        for r in range(1, SEQ):
            give_back(c, r).wait_recv()
        gate = mod_ref[c, 2:3, :]
        for f in range(TL):
            a = got[c, f].astype(F32).reshape(SEQ * PL, QK).astype(BF16)
            p = nn(a, wot[...])
            live = jnp.where(TL * s_me + f < cf_ref[c], 1.0, 0.0)
            res = held[c, f].astype(F32).reshape(SEQ * PL, D) + (live * gate) * p
            outv[c, f] = res.reshape(SEQ, PL, D).astype(BF16)
            out_copy(c, f).start()

    for r in range(1, NY):
        piece(r).wait_send()
    for c in range(C):
        for r in range(1, SEQ):
            forth(c, r).wait_send()
            give_back(c, r).wait_send()
    for kind in range(2):
        for r in range(1, NZ):
            z_copy(kind, r).wait_send()
        for way in range(3):
            for k in range(NZ):
                x_copy(kind, way, k, x, z, right).wait_send()
    for xr in range(NX):
        core_copy_o(xr).wait_send()
        for k in range(NZ):
            core_copy_q(xr, k).wait_send()
    for c in range(C):
        for f in range(TL):
            out_copy(c, f).wait()


def shards(latents, modulation, w_qkv, w_out, clip_frames, time_positions):
    vmem = pl.BlockSpec(memory_space=pltpu.VMEM)
    smem = pl.BlockSpec(memory_space=pltpu.SMEM)
    hbm = pl.BlockSpec(memory_space=pl.ANY)
    dma = pltpu.SemaphoreType.DMA
    grouped = latents.reshape(C, TL, SEQ, PL, D)
    out = pl.pallas_call(
        kernel,
        out_shape=jax.ShapeDtypeStruct(grouped.shape, BF16),
        in_specs=[hbm, vmem, vmem, vmem, smem, smem],
        out_specs=hbm,
        scratch_shapes=[
            pltpu.VMEM((C, SEQ, TL, PL, D), BF16),
            pltpu.VMEM((C, TOK, D), BF16),
            pltpu.VMEM((NX, NZ, 3, 16, 128), BF16),
            pltpu.VMEM((2, NY, NX, NZ, 3, 16, 128), BF16),
            pltpu.VMEM((3 * QK, D), BF16),
            pltpu.VMEM((QK, D), BF16),
            pltpu.VMEM((3 * QK, TOK), BF16),
            pltpu.VMEM((QK, TOK), BF16),
            pltpu.VMEM((C, SEQ, TL, PL, QK), BF16),
            pltpu.VMEM((C, TL, SEQ, PL, QK), BF16),
            pltpu.VMEM((C, TL, SEQ, PL, D), BF16),
            pltpu.VMEM((C, TL, SEQ, PL, D), BF16),
            pltpu.VMEM((C, HP, TOK), F32),
            pltpu.VMEM((C, HP, TOK), F32),
            pltpu.VMEM((C, HP, TOK), F32),
            pltpu.VMEM((C, TOK, TOK), BF16),
            dma((NY,)), dma((NY,)),
            dma((2, NZ)), dma((2, NZ)),
            dma((2, 3, NZ)), dma((2, 3, NZ)),
            dma((NX, NZ)), dma((NX, NZ)),
            dma((NX,)), dma((NX,)),
            dma((C, SEQ)), dma((C, SEQ)),
            dma((C, SEQ)), dma((C, SEQ)),
            dma((C,)), dma, dma((C, TL)),
        ],
        compiler_params=pltpu.CompilerParams(
            collective_id=0, has_side_effects=True, vmem_limit_bytes=56 * 1024 * 1024
        ),
        cost_estimate=pl.CostEstimate(flops=6 * 10**9, bytes_accessed=8 * 10**6, transcendentals=10**7),
    )(grouped, modulation, w_qkv.T, w_out, clip_frames, time_positions)
    return out.reshape(latents.shape)


def solution(mesh):
    return jax.shard_map(
        shards,
        mesh=mesh,
        in_specs=(
            P("dp", "seq", None, None),
            P("dp", None, None),
            P(None, "seq"),
            P("seq", None),
            P("dp"),
            P("dp", None),
        ),
        out_specs=P("dp", "seq", None, None),
        check_vma=False,
    )
```

```python
import functools
import math

import jax
import jax.numpy as jnp
from jax import lax
from jax.experimental import pallas as pl
from jax.experimental.pallas import tpu as pltpu
from jax.sharding import PartitionSpec as P

MESH = pl.DeviceIdType.MESH
F32 = jnp.float32
BF16 = jnp.bfloat16

D = 1152
H = 8
HD = 72
C = 2
T = 48
SEQ = 16
NX = 4
NZ = 8
NY = 8
TL = 3
PL = 8
TOK = T * PL
HP = 80
QK = H * HP
VD = H * HD
BACK = 14
KT = D // 128
ZREL = (0, 1, 7, 2, 6, 3, 5, 4)


def nt(a, b):
    return lax.dot_general(a, b, (((1,), (1,)), ((), ())), preferred_element_type=F32)


def nn(a, b):
    return lax.dot_general(a, b, (((1,), (0,)), ((), ())), preferred_element_type=F32)


def row_ids(shape):
    return lax.broadcasted_iota(jnp.int32, shape, 0)


def lane_ids(shape):
    return lax.broadcasted_iota(jnp.int32, shape, 1)


def normalise(xin, xm, mod_ref, c):
    @pl.loop(0, SEQ // 2)
    def _(k):
        v = xin[c, pl.ds(2 * k, 2)].astype(F32).reshape(2 * TL * PL, D)
        mean = jnp.mean(v, axis=-1, keepdims=True)
        v = v - mean
        var = jnp.mean(v * v, axis=-1, keepdims=True)
        normed = v * lax.rsqrt(var + 1e-6)
        shift = mod_ref[0, c : c + 1, :]
        scale = mod_ref[1, c : c + 1, :]
        rows = pl.ds(pl.multiple_of(48 * k, 48), 48)
        xm[c, rows, :] = (normed * (1.0 + scale) + shift).astype(BF16)


def tables(tp_ref, cf_ref, cos_t, even_t, odd_t, mask_t):
    shape = (HP, TOK)
    r = row_ids(shape)
    pair = lax.shift_right_logical(r, 1)
    freq = jnp.exp(pair.astype(F32) * (-math.log(10000.0) * 2.0 / HD))
    is_even = (r & 1) == 0
    frame = lax.shift_right_logical(lane_ids((8, TOK)), 3)
    key = row_ids((TOK, TOK))
    query = lane_ids((TOK, TOK))
    same = (key & 7) == (query & 7)
    key_frame = lax.shift_right_logical(key, 3)
    for c in range(C):
        pos = jnp.zeros((8, TOK), F32)
        for t in range(T):
            pos = jnp.where(frame == t, tp_ref[c, t].astype(F32), pos)
        angle = freq * pos[0:1]
        sine = jnp.sin(angle)
        cos_t[c] = jnp.cos(angle)
        even_t[c] = jnp.where(is_even, -sine, 0.0)
        odd_t[c] = jnp.where(is_even, 0.0, sine)
        live = same & (key_frame < cf_ref[c])
        mask_t[c] = jnp.where(live, 1.0, 0.0).astype(BF16)


def pack_weights(wq_ref, wo_ref, wloc):
    for i in range(64):
        d, j = divmod(i, 2)
        kt, rt = divmod(i, 7)
        if kt < KT and rt < 6:
            tile = wq_ref[16 * rt : 16 * rt + 16, 128 * kt : 128 * kt + 128]
        elif kt < KT:
            part = wq_ref[96:108, 128 * kt : 128 * kt + 128].astype(F32)
            tile = jnp.concatenate([part, jnp.zeros((4, 128), F32)], axis=0).astype(BF16)
        else:
            tile = jnp.zeros((16, 128), BF16)
        wloc[d // NZ, d % NZ, j] = tile
    for d in range(32):
        kt, rt = divmod(d, 3)
        if kt < KT and rt < 2:
            tile = wo_ref[16 * rt : 16 * rt + 16, 128 * kt : 128 * kt + 128]
        elif kt < KT:
            part = wo_ref[32:36, 128 * kt : 128 * kt + 128].astype(F32)
            tile = jnp.concatenate([part, jnp.zeros((12, 128), F32)], axis=0).astype(BF16)
        else:
            tile = jnp.zeros((16, 128), BF16)
        wloc[d // NZ, d % NZ, 2] = tile


def join(first, second, rows):
    second = pltpu.roll(second, 4, 0)
    cut = rows - 4
    return jnp.concatenate([first[:cut], first[cut : cut + 8] + second[:8], second[8 : rows + 4]], axis=0)


def unpack_qkv(g, wt):
    @pl.loop(0, NY)
    def _(y):
        for kt in range(KT):
            shard = []
            for core in range(2):
                tiles = []
                for i in range(7 * kt, 7 * kt + 7):
                    d, j = divmod(i, 2)
                    tiles.append(g[core, y, d // NZ, d % NZ, j].astype(F32))
                shard.append(jnp.concatenate(tiles, axis=0))
            w = join(shard[0], shard[1], 108)
            gap = jnp.zeros((8, 128), F32)
            rows = [w[0:72], gap, w[72:144], gap, w[144:216], gap]
            block = jnp.concatenate(rows, axis=0).astype(BF16)
            wt[pl.ds(pl.multiple_of(240 * y, 240), 240), 128 * kt : 128 * kt + 128] = block


def unpack_out(go, wot):
    @pl.loop(0, NY // 2)
    def _(i):
        for kt in range(KT):
            rows = []
            for j in range(2):
                shard = []
                for core in range(2):
                    tiles = []
                    for d in range(3 * kt, 3 * kt + 3):
                        tiles.append(go[core, d // NZ, d % NZ, 2 * i + j].astype(F32))
                    shard.append(jnp.concatenate(tiles, axis=0))
                rows.append(join(shard[0], shard[1], 36))
            block = jnp.concatenate(rows, axis=0).astype(BF16)
            wot[pl.ds(pl.multiple_of(144 * i, 144), 144), 128 * kt : 128 * kt + 128] = block

    wot[VD : VD + 128] = jnp.zeros((128, D), BF16)
    wot[VD + 128 : VD + 192] = wot[VD - 64 : VD]


def rotate(v, cos, even, odd):
    total = jnp.sum(v * v, axis=0, keepdims=True)
    v = v * lax.rsqrt(total * (1.0 / HD) + 1e-6)
    up = pltpu.roll(v, HP - 1, 0)
    down = pltpu.roll(v, 1, 0)
    return (v * cos + up * even + down * odd).astype(BF16)


def attend(c, part, xm, wt, qkv_t, att_t, back, cos_t, even_t, odd_t, mask_t):
    x = xm[c]
    for block in range(3):
        first = QK * block + QK // 2 * part
        rows = slice(first, first + QK // 2)
        qkv_t[rows, :] = nt(wt[rows, :], x).astype(BF16)

    ones_row = jnp.where(row_ids((HP, 1)) == HD, 1.0, 0.0).astype(BF16)
    for h in range(4 * part, 4 * part + 4):
        rows = HP * h
        cos, even, odd = cos_t[c], even_t[c], odd_t[c]
        q = rotate(qkv_t[rows : rows + HP].astype(F32), cos, even, odd)
        k = rotate(qkv_t[QK + rows : QK + rows + HP].astype(F32), cos, even, odd)
        v = qkv_t[2 * QK + rows : 2 * QK + rows + HP] + ones_row
        s = nn(k.T, q)
        e = jnp.exp(s * (1.0 / math.sqrt(HD))).astype(BF16) * mask_t[c]
        o = nn(v, e)
        att_t[HD * h : HD * h + HD] = o[:HD] / o[HD : HD + 1]
    for j in (2 * part, 2 * part + 1):
        turned = att_t[128 * j : 128 * j + 128].T.reshape(SEQ, TL, PL, 128)
        back[c, :, 3 * j : 3 * j + 3] = turned.astype(BF16)
    if part:
        last = att_t[VD - 64 : VD]
        turned = jnp.concatenate([last, last], axis=0).T.reshape(SEQ, TL, PL, 128)
        lane = lax.broadcasted_iota(jnp.int32, (SEQ, PL, 128), 2)
        back[c, :, 12] = jnp.where(lane < 64, turned[:, 0], turned[:, 1]).astype(BF16)
        back[c, :, 13] = turned[:, 2].astype(BF16)


def kernel(
    lat, mod_in, wq_in, wo_in, cf_ref, tp_ref, out,
    mod_ref, wq_ref, wo_ref, xin, xm, wloc, g, go, wt, wot, qkv_t, att_t, back, got, held, outv, cos_t, even_t, odd_t, mask_t,
    a_s, a_r, z_s, z_r, x_s, x_r, cq_s, cq_r, oz_s, oz_r, ox_s, ox_r, co_s, co_r, f_s, f_r, r_s, r_r, own_sem, in_sem, held_sem, out_sem,
):
    s_me = lax.axis_index("seq")
    d_me = lax.axis_index("dp")
    y, core = s_me // 2, s_me % 2
    z, x = d_me // NX, d_me % NX

    def seq_id(s):
        return (s, d_me)

    def plane_id(zz, xx):
        return (s_me, zz * NX + xx)

    sibling = seq_id(s_me + 1 - 2 * core)

    def remote(src, dst, send, recv, to):
        return pltpu.make_async_remote_copy(
            src_ref=src, dst_ref=dst, send_sem=send, recv_sem=recv, device_id=to, device_id_type=MESH
        )

    barrier = pltpu.get_barrier_semaphore()
    for r in range(1, SEQ):
        pl.semaphore_signal(barrier, inc=1, device_id=seq_id((s_me + r) % SEQ), device_id_type=MESH)
    z_next = (plane_id((z + 1) % NZ, x), plane_id((z + NZ - 1) % NZ, x))
    x_next = (plane_id(z, (x + 1) % NX), plane_id(z, (x + NX - 1) % NX))
    for r in range(1, NZ):
        pl.semaphore_signal(barrier, inc=1, device_id=plane_id((z + r) % NZ, x), device_id_type=MESH)
    for r in range(1, NX):
        pl.semaphore_signal(barrier, inc=1, device_id=plane_id(z, (x + r) % NX), device_id_type=MESH)

    loads = [
        pltpu.make_async_copy(wq_in, wq_ref, in_sem.at[0]),
        pltpu.make_async_copy(wo_in, wo_ref, in_sem.at[1]),
        pltpu.make_async_copy(mod_in, mod_ref, in_sem.at[2]),
    ]
    for copy in loads:
        copy.start()
    own = [pltpu.make_async_copy(lat.at[c, :, s_me], xin.at[c, s_me], own_sem.at[c]) for c in range(C)]
    for c in range(C):
        own[c].start()
    hold = pltpu.make_async_copy(lat, held, held_sem)
    hold.start()
    for copy in loads[:2]:
        copy.wait()
    pack_weights(wq_ref, wo_ref, wloc)
    g[core, y, x, z] = wloc[x, z]
    pl.semaphore_wait(barrier, SEQ - 1 + NZ - 1 + NX - 1)

    def piece(r):
        yy = (y + r) % NY
        return remote(wloc.at[x, z], g.at[core, y, x, z], a_s.at[r], a_r.at[r], seq_id(2 * yy + core))

    for r in (1, 7, 2, 6, 3, 5, 4):
        piece(r).start()

    def forth(c, r):
        to = (s_me + r) % SEQ
        return remote(lat.at[c, :, to], xin.at[c, s_me], f_s.at[c, r], f_r.at[c, r], seq_id(to))

    for r in (1, 15, 2, 14, 3, 13, 4, 12, 5, 11, 6, 10, 7, 9, 8):
        forth(0, r).start()

    half = (slice(0, NY // 2), slice(NY // 2, NY))
    tiles = slice(0, 2)

    def z_copy(way, m):
        zz = (z + (NZ - m if way == 0 else m) + 1 - 2 * way) % NZ
        ys = half[way] if m == NZ // 2 else slice(None)
        block = g.at[core, ys, x, zz, tiles]
        return remote(block, block, z_s.at[way, m], z_r.at[way, m], z_next[way])

    def x_copy(way, k, behind):
        xx = (x + (NX - behind if way == 0 else behind) + 1 - 2 * way) % NX
        block = g.at[core, :, xx, (z + ZREL[k]) % NZ, tiles]
        n = 2 * (behind - 1) + way
        return remote(block, block, x_s.at[n, k], x_r.at[n, k], x_next[way])

    def core_copy(xr, k):
        block = g.at[core, :, (x + xr) % NX, (z + ZREL[k]) % NZ, tiles]
        return remote(block, block, cq_s.at[xr, k], cq_r.at[xr, k], sibling)

    def column(k):
        x_copy(0, k, 1).start()
        x_copy(1, k, 1).start()
        core_copy(0, k).start()

    def z_step(m):
        for way in range(2):
            z_copy(way, m).wait_recv()
            if m < NZ // 2:
                z_copy(way, m + 1).start()
                column(2 * m - way)
        if m == NZ // 2:
            column(7)

    def x_step(k):
        for way in (k % 2, 1 - k % 2):
            x_copy(way, k, 1).wait_recv()
            if way == k % 2:
                x_copy(way, k, 2).start()
            core_copy((3, 1)[way], k).start()

    def x_across(k):
        x_copy(k % 2, k, 2).wait_recv()
        core_copy(2, k).start()

    def oz_copy(r):
        mine = g.at[core, :, x, z, 2]
        return remote(mine, go.at[core, x, z], oz_s.at[r], oz_r.at[r], plane_id((z + r) % NZ, x))

    def ox_copy(r):
        block = go.at[core, x]
        return remote(block, block, ox_s.at[r], ox_r.at[r], plane_id(z, (x + r) % NX))

    def o_core_copy(xr):
        block = go.at[core, (x + xr) % NX]
        return remote(block, block, co_s.at[xr], co_r.at[xr], sibling)

    for r in (1, 7, 2, 6, 3, 5, 4):
        piece(r).wait_recv()
    for way in range(2):
        z_copy(way, 1).start()
    column(0)
    for r in (1, 15, 2, 14, 3, 13, 4, 12, 5, 11, 6, 10, 7, 9, 8):
        forth(1, r).start()
    tables(tp_ref, cf_ref, cos_t, even_t, odd_t, mask_t)

    steps = [(2.4 * m, z_step, m) for m in range(1, 5)]
    steps += [(2.6 + 2.1 * k, x_step, k) for k in range(NZ)]
    steps += [(5.0 + 2.1 * k, x_across, k) for k in range(NZ)]
    for _, step, at in sorted(steps, key=lambda e: e[0]):
        step(at)
        if step is z_step and at == 3:
            go[core, x, z] = g[core, :, x, z, 2]
            for r in (1, 7, 2, 6, 3, 5, 4):
                oz_copy(r).start()
    for r in range(1, NZ):
        oz_copy(r).wait_recv()
    for r in (1, 3, 2):
        ox_copy(r).start()
    o_core_copy(0).start()

    def arrived(c):
        own[c].wait()
        for r in range(1, SEQ):
            forth(c, r).wait_recv()

    parts = (slice(0, 6), slice(6, BACK))

    def give_back(c, part, r):
        to = (s_me + r) % SEQ
        return remote(
            back.at[c, to, parts[part]], got.at[c, s_me, parts[part]], r_s.at[c, part, r], r_r.at[c, part, r], seq_id(to)
        )

    def keep(c):
        return pltpu.make_async_copy(back.at[c, s_me], got.at[c, s_me], own_sem.at[c])

    def clip(c):
        for part in range(2):
            attend(c, part, xm, wt, qkv_t, att_t, back, cos_t, even_t, odd_t, mask_t)
            for r in (1, 15, 2, 14, 3, 13, 4, 12, 5, 11, 6, 10, 7, 9, 8):
                give_back(c, part, r).start()
        keep(c).start()

    arrived(0)
    loads[2].wait()
    normalise(xin, xm, mod_ref, 0)
    for k in range(NZ):
        for xr in range(NX):
            core_copy(xr, k).wait_recv()
    unpack_qkv(g, wt)

    clip(0)
    for r in (1, 3, 2):
        ox_copy(r).wait_recv()
        o_core_copy(NX - r).start()
    arrived(1)
    normalise(xin, xm, mod_ref, 1)
    clip(1)
    for xr in range(NX):
        o_core_copy(xr).wait_recv()
    unpack_out(go, wot)
    hold.wait()

    def out_copy(c, f):
        return pltpu.make_async_copy(outv.at[c, f], out.at[c, f], out_sem.at[c, f])

    for c in range(C):
        keep(c).wait()
        for part in range(2):
            for r in range(1, SEQ):
                give_back(c, part, r).wait_recv()
        gate = mod_ref[2, c : c + 1, :]
        for f in range(TL):
            lanes = [got[c, :, at].astype(F32).reshape(SEQ * PL, 128) for at in (f, 3 + f, 6 + f, 9 + f, 12 + f // 2)]
            if f == 1:
                a = jnp.concatenate(lanes[:4], axis=1).astype(BF16)
                p = nn(a, wot[:512]) + nn(lanes[4].astype(BF16), wot[VD + 64 : VD + 192])
            else:
                p = nn(jnp.concatenate(lanes, axis=1).astype(BF16), wot[: VD + 64])
            live = jnp.where(TL * s_me + f < cf_ref[c], 1.0, 0.0)
            res = held[c, f].astype(F32).reshape(SEQ * PL, D) + (live * gate) * p
            outv[c, f] = res.reshape(SEQ, PL, D).astype(BF16)
            out_copy(c, f).start()

    for r in range(1, NY):
        piece(r).wait_send()
    for c in range(C):
        for r in range(1, SEQ):
            forth(c, r).wait_send()
            for part in range(2):
                give_back(c, part, r).wait_send()
    for way in range(2):
        for m in range(1, NZ // 2 + 1):
            z_copy(way, m).wait_send()
        for k in range(NZ):
            x_copy(way, k, 1).wait_send()
    for k in range(NZ):
        x_copy(k % 2, k, 2).wait_send()
    for r in range(1, NZ):
        oz_copy(r).wait_send()
    for r in range(1, NX):
        ox_copy(r).wait_send()
    for xr in range(NX):
        o_core_copy(xr).wait_send()
        for k in range(NZ):
            core_copy(xr, k).wait_send()
    for c in range(C):
        for f in range(TL):
            out_copy(c, f).wait()


def shards(latents, modulation, w_qkv, w_out, clip_frames, time_positions):
    smem = pl.BlockSpec(memory_space=pltpu.SMEM)
    hbm = pl.BlockSpec(memory_space=pl.ANY)
    dma = pltpu.SemaphoreType.DMA
    grouped = latents.reshape(C, TL, SEQ, PL, D)
    out = pl.pallas_call(
        kernel,
        out_shape=jax.ShapeDtypeStruct(grouped.shape, BF16),
        in_specs=[hbm, hbm, hbm, hbm, smem, smem],
        out_specs=hbm,
        scratch_shapes=[
            pltpu.VMEM((3, C, D), F32),
            pltpu.VMEM((3 * VD // SEQ, D), BF16),
            pltpu.VMEM((VD // SEQ, D), BF16),
            pltpu.VMEM((C, SEQ, TL, PL, D), BF16),
            pltpu.VMEM((C, TOK, D), BF16),
            pltpu.VMEM((NX, NZ, 3, 16, 128), BF16),
            pltpu.VMEM((2, NY, NX, NZ, 3, 16, 128), BF16),
            pltpu.VMEM((2, NX, NZ, NY, 16, 128), BF16),
            pltpu.VMEM((3 * QK, D), BF16),
            pltpu.VMEM((VD + 192, D), BF16),
            pltpu.VMEM((3 * QK, TOK), BF16),
            pltpu.VMEM((VD, TOK), F32),
            pltpu.VMEM((C, SEQ, BACK, PL, 128), BF16),
            pltpu.VMEM((C, SEQ, BACK, PL, 128), BF16),
            pltpu.VMEM((C, TL, SEQ, PL, D), BF16),
            pltpu.VMEM((C, TL, SEQ, PL, D), BF16),
            pltpu.VMEM((C, HP, TOK), F32),
            pltpu.VMEM((C, HP, TOK), F32),
            pltpu.VMEM((C, HP, TOK), F32),
            pltpu.VMEM((C, TOK, TOK), BF16),
            dma((NY,)), dma((NY,)),
            dma((2, 5)), dma((2, 5)),
            dma((4, NZ)), dma((4, NZ)),
            dma((NX, NZ)), dma((NX, NZ)),
            dma((NZ,)), dma((NZ,)),
            dma((NX,)), dma((NX,)),
            dma((NX,)), dma((NX,)),
            dma((C, SEQ)), dma((C, SEQ)),
            dma((C, 2, SEQ)), dma((C, 2, SEQ)),
            dma((C,)), dma((3,)), dma, dma((C, TL)),
        ],
        compiler_params=pltpu.CompilerParams(
            collective_id=0, has_side_effects=True, vmem_limit_bytes=56 * 1024 * 1024
        ),
        cost_estimate=pl.CostEstimate(flops=6 * 10**9, bytes_accessed=8 * 10**6, transcendentals=10**7),
    )(grouped, modulation.transpose(1, 0, 2), w_qkv.T, w_out, clip_frames, time_positions)
    return out.reshape(latents.shape)


def solution(mesh):
    return jax.shard_map(
        shards,
        mesh=mesh,
        in_specs=(
            P("dp", "seq", None, None),
            P("dp", None, None),
            P(None, "seq"),
            P("seq", None),
            P("dp"),
            P("dp", None),
        ),
        out_specs=P("dp", "seq", None, None),
        check_vma=False,
    )
```

```python
import functools
import math

import jax
import jax.numpy as jnp
from jax import lax
from jax.experimental import pallas as pl
from jax.experimental.pallas import tpu as pltpu
from jax.sharding import PartitionSpec as P

MESH = pl.DeviceIdType.MESH
F32 = jnp.float32
BF16 = jnp.bfloat16

D = 1152
H = 8
HD = 72
C = 2
T = 48
SEQ = 16
NX = 4
NZ = 8
NY = 8
TL = 3
PL = 8
TOK = T * PL
HP = 80
QK = H * HP
VD = H * HD
BACK = 14
KT = D // 128
ZREL = (0, 1, 7, 2, 6, 3, 5, 4)
NEAR_SEQ = (1, 15, 2, 14, 3, 13, 4, 12, 5, 11, 6, 10, 7, 9, 8)
FAR_SEQ = NEAR_SEQ[::-1]
NEAR_EIGHT = (1, 7, 2, 6, 3, 5, 4)


def nt(a, b):
    return lax.dot_general(a, b, (((1,), (1,)), ((), ())), preferred_element_type=F32)


def nn(a, b):
    return lax.dot_general(a, b, (((1,), (0,)), ((), ())), preferred_element_type=F32)


def row_ids(shape):
    return lax.broadcasted_iota(jnp.int32, shape, 0)


def lane_ids(shape):
    return lax.broadcasted_iota(jnp.int32, shape, 1)


def normalise(xin, xm, mod_ref, c):
    @pl.loop(0, SEQ // 2)
    def _(k):
        v = xin[c, pl.ds(2 * k, 2)].astype(F32).reshape(2 * TL * PL, D)
        mean = jnp.mean(v, axis=-1, keepdims=True)
        v = v - mean
        var = jnp.mean(v * v, axis=-1, keepdims=True)
        normed = v * lax.rsqrt(var + 1e-6)
        shift = mod_ref[0, c : c + 1, :]
        scale = mod_ref[1, c : c + 1, :]
        rows = pl.ds(pl.multiple_of(48 * k, 48), 48)
        xm[c, rows, :] = (normed * (1.0 + scale) + shift).astype(BF16)


def tables(tp_ref, cf_ref, cos_t, even_t, odd_t, mask_t):
    shape = (HP, TOK)
    r = row_ids(shape)
    pair = lax.shift_right_logical(r, 1)
    freq = jnp.exp(pair.astype(F32) * (-math.log(10000.0) * 2.0 / HD))
    is_even = (r & 1) == 0
    frame = lax.shift_right_logical(lane_ids((8, TOK)), 3)
    key = row_ids((TOK, TOK))
    query = lane_ids((TOK, TOK))
    same = (key & 7) == (query & 7)
    key_frame = lax.shift_right_logical(key, 3)
    for c in range(C):
        pos = jnp.zeros((8, TOK), F32)
        for t in range(T):
            pos = jnp.where(frame == t, tp_ref[c, t].astype(F32), pos)
        angle = freq * pos[0:1]
        sine = jnp.sin(angle)
        cos_t[c] = jnp.cos(angle)
        even_t[c] = jnp.where(is_even, -sine, 0.0)
        odd_t[c] = jnp.where(is_even, 0.0, sine)
        live = same & (key_frame < cf_ref[c])
        mask_t[c] = jnp.where(live, 1.0, 0.0).astype(BF16)


def pack_weights(wq_ref, wo_ref, wloc):
    for i in range(64):
        d, j = divmod(i, 2)
        kt, rt = divmod(i, 7)
        if kt < KT and rt < 6:
            tile = wq_ref[16 * rt : 16 * rt + 16, 128 * kt : 128 * kt + 128]
        elif kt < KT:
            part = wq_ref[96:108, 128 * kt : 128 * kt + 128].astype(F32)
            tile = jnp.concatenate([part, jnp.zeros((4, 128), F32)], axis=0).astype(BF16)
        else:
            tile = jnp.zeros((16, 128), BF16)
        wloc[d // NZ, d % NZ, j] = tile
    for d in range(32):
        kt, rt = divmod(d, 3)
        if kt < KT and rt < 2:
            tile = wo_ref[16 * rt : 16 * rt + 16, 128 * kt : 128 * kt + 128]
        elif kt < KT:
            part = wo_ref[32:36, 128 * kt : 128 * kt + 128].astype(F32)
            tile = jnp.concatenate([part, jnp.zeros((12, 128), F32)], axis=0).astype(BF16)
        else:
            tile = jnp.zeros((16, 128), BF16)
        wloc[d // NZ, d % NZ, 2] = tile


def join(first, second, rows):
    second = pltpu.roll(second, 4, 0)
    cut = rows - 4
    return jnp.concatenate([first[:cut], first[cut : cut + 8] + second[:8], second[8 : rows + 4]], axis=0)


def unpack_qkv(g, wt):
    @pl.loop(0, NY)
    def _(y):
        for kt in range(KT):
            shard = []
            for core in range(2):
                tiles = []
                for i in range(7 * kt, 7 * kt + 7):
                    d, j = divmod(i, 2)
                    tiles.append(g[core, y, d // NZ, d % NZ, j].astype(F32))
                shard.append(jnp.concatenate(tiles, axis=0))
            w = join(shard[0], shard[1], 108)
            gap = jnp.zeros((8, 128), F32)
            rows = [w[0:72], gap, w[72:144], gap, w[144:216], gap]
            block = jnp.concatenate(rows, axis=0).astype(BF16)
            wt[pl.ds(pl.multiple_of(240 * y, 240), 240), 128 * kt : 128 * kt + 128] = block


def unpack_out(go, wot):
    @pl.loop(0, NY // 2)
    def _(i):
        for kt in range(KT):
            rows = []
            for j in range(2):
                shard = []
                for core in range(2):
                    tiles = []
                    for d in range(3 * kt, 3 * kt + 3):
                        tiles.append(go[core, d // NZ, d % NZ, 2 * i + j].astype(F32))
                    shard.append(jnp.concatenate(tiles, axis=0))
                rows.append(join(shard[0], shard[1], 36))
            block = jnp.concatenate(rows, axis=0).astype(BF16)
            wot[pl.ds(pl.multiple_of(144 * i, 144), 144), 128 * kt : 128 * kt + 128] = block

    wot[VD : VD + 128] = jnp.zeros((128, D), BF16)
    wot[VD + 128 : VD + 192] = wot[VD - 64 : VD]


def rotate(v, cos, even, odd):
    total = jnp.sum(v * v, axis=0, keepdims=True)
    v = v * lax.rsqrt(total * (1.0 / HD) + 1e-6)
    up = pltpu.roll(v, HP - 1, 0)
    down = pltpu.roll(v, 1, 0)
    return (v * cos + up * even + down * odd).astype(BF16)


def attend(c, part, xm, wt, qkv_t, att_t, back, cos_t, even_t, odd_t, mask_t):
    x = xm[c]
    for block in range(3):
        first = QK * block + QK // 2 * part
        rows = slice(first, first + QK // 2)
        qkv_t[rows, :] = nt(wt[rows, :], x).astype(BF16)

    ones_row = jnp.where(row_ids((HP, 1)) == HD, 1.0, 0.0).astype(BF16)
    for h in range(4 * part, 4 * part + 4):
        rows = HP * h
        cos, even, odd = cos_t[c], even_t[c], odd_t[c]
        q = rotate(qkv_t[rows : rows + HP].astype(F32), cos, even, odd)
        k = rotate(qkv_t[QK + rows : QK + rows + HP].astype(F32), cos, even, odd)
        v = qkv_t[2 * QK + rows : 2 * QK + rows + HP] + ones_row
        s = nn(k.T, q)
        e = jnp.exp(s * (1.0 / math.sqrt(HD))).astype(BF16) * mask_t[c]
        o = nn(v, e)
        att_t[HD * h : HD * h + HD] = o[:HD] / o[HD : HD + 1]
    for j in (2 * part, 2 * part + 1):
        turned = att_t[128 * j : 128 * j + 128].T.reshape(SEQ, TL, PL, 128)
        back[c, :, 3 * j : 3 * j + 3] = turned.astype(BF16)
    if part:
        last = att_t[VD - 64 : VD]
        turned = jnp.concatenate([last, last], axis=0).T.reshape(SEQ, TL, PL, 128)
        lane = lax.broadcasted_iota(jnp.int32, (SEQ, PL, 128), 2)
        back[c, :, 12] = jnp.where(lane < 64, turned[:, 0], turned[:, 1]).astype(BF16)
        back[c, :, 13] = turned[:, 2].astype(BF16)


def kernel(
    lat, mod_in, wq_in, wo_in, cf_ref, tp_ref, out,
    mod_ref, wq_ref, wo_ref, xin, xm, wloc, g, go, wt, wot, qkv_t, att_t, back, got, held, outv, cos_t, even_t, odd_t, mask_t,
    a_s, a_r, z_s, z_r, x_s, x_r, cq_s, cq_r, oz_s, oz_r, ox_s, ox_r, co_s, co_r, f_s, f_r, r_s, r_r, own_sem, in_sem, held_sem, out_sem,
):
    s_me = lax.axis_index("seq")
    d_me = lax.axis_index("dp")
    y, core = s_me // 2, s_me % 2
    z, x = d_me // NX, d_me % NX

    def seq_id(s):
        return (s, d_me)

    def plane_id(zz, xx):
        return (s_me, zz * NX + xx)

    sibling = seq_id(s_me + 1 - 2 * core)

    def remote(src, dst, send, recv, to):
        return pltpu.make_async_remote_copy(
            src_ref=src, dst_ref=dst, send_sem=send, recv_sem=recv, device_id=to, device_id_type=MESH
        )

    barrier = pltpu.get_barrier_semaphore()
    for r in range(1, SEQ):
        pl.semaphore_signal(barrier, inc=1, device_id=seq_id((s_me + r) % SEQ), device_id_type=MESH)
    z_next = (plane_id((z + 1) % NZ, x), plane_id((z + NZ - 1) % NZ, x))
    x_next = (plane_id(z, (x + 1) % NX), plane_id(z, (x + NX - 1) % NX))
    for r in range(1, NZ):
        pl.semaphore_signal(barrier, inc=1, device_id=plane_id((z + r) % NZ, x), device_id_type=MESH)
    for r in range(1, NX):
        pl.semaphore_signal(barrier, inc=1, device_id=plane_id(z, (x + r) % NX), device_id_type=MESH)

    loads = [
        pltpu.make_async_copy(wq_in, wq_ref, in_sem.at[0]),
        pltpu.make_async_copy(wo_in, wo_ref, in_sem.at[1]),
        pltpu.make_async_copy(mod_in, mod_ref, in_sem.at[2]),
    ]
    for copy in loads:
        copy.start()
    own = [pltpu.make_async_copy(lat.at[c, :, s_me], xin.at[c, s_me], own_sem.at[c]) for c in range(C)]
    for c in range(C):
        own[c].start()
    hold = pltpu.make_async_copy(lat, held, held_sem)
    for copy in loads[:2]:
        copy.wait()
    pack_weights(wq_ref, wo_ref, wloc)
    g[core, y, x, z] = wloc[x, z]
    pl.semaphore_wait(barrier, SEQ - 1 + NZ - 1 + NX - 1)

    def piece(r):
        yy = (y + r) % NY
        return remote(wloc.at[x, z], g.at[core, y, x, z], a_s.at[r], a_r.at[r], seq_id(2 * yy + core))

    for r in NEAR_EIGHT:
        piece(r).start()

    def forth(c, r):
        to = (s_me + r) % SEQ
        return remote(lat.at[c, :, to], xin.at[c, s_me], f_s.at[c, r], f_r.at[c, r], seq_id(to))

    for r in NEAR_SEQ:
        forth(0, r).start()

    half = (slice(0, NY // 2), slice(NY // 2, NY))
    tiles = slice(0, 2)

    def z_copy(way, m):
        zz = (z + (NZ - m if way == 0 else m) + 1 - 2 * way) % NZ
        ys = half[way] if m == NZ // 2 else slice(None)
        block = g.at[core, ys, x, zz, tiles]
        return remote(block, block, z_s.at[way, m], z_r.at[way, m], z_next[way])

    def x_copy(way, k, behind):
        xx = (x + (NX - behind if way == 0 else behind) + 1 - 2 * way) % NX
        block = g.at[core, :, xx, (z + ZREL[k]) % NZ, tiles]
        n = 2 * (behind - 1) + way
        return remote(block, block, x_s.at[n, k], x_r.at[n, k], x_next[way])

    def core_copy(xr, k):
        block = g.at[core, :, (x + xr) % NX, (z + ZREL[k]) % NZ, tiles]
        return remote(block, block, cq_s.at[xr, k], cq_r.at[xr, k], sibling)

    def column(k):
        x_copy(0, k, 1).start()
        x_copy(1, k, 1).start()
        core_copy(0, k).start()

    def z_step(m):
        for way in range(2):
            z_copy(way, m).wait_recv()
            if m < NZ // 2:
                z_copy(way, m + 1).start()
                column(2 * m - way)
        if m == NZ // 2:
            column(7)

    def x_step(k):
        for way in (k % 2, 1 - k % 2):
            x_copy(way, k, 1).wait_recv()
            if way == k % 2:
                x_copy(way, k, 2).start()
            core_copy((3, 1)[way], k).start()

    def x_across(k):
        x_copy(k % 2, k, 2).wait_recv()
        core_copy(2, k).start()

    def oz_copy(r):
        mine = g.at[core, :, x, z, 2]
        return remote(mine, go.at[core, x, z], oz_s.at[r], oz_r.at[r], plane_id((z + r) % NZ, x))

    def ox_copy(r):
        block = go.at[core, x]
        return remote(block, block, ox_s.at[r], ox_r.at[r], plane_id(z, (x + r) % NX))

    def o_core_copy(xr):
        block = go.at[core, (x + xr) % NX]
        return remote(block, block, co_s.at[xr], co_r.at[xr], sibling)

    for r in NEAR_EIGHT:
        piece(r).wait_recv()
    for way in range(2):
        z_copy(way, 1).start()
    column(0)
    for r in NEAR_SEQ:
        forth(1, r).start()
    tables(tp_ref, cf_ref, cos_t, even_t, odd_t, mask_t)

    steps = [(2.4 * m, z_step, m) for m in range(1, 5)]
    steps += [(2.6 + 2.1 * k, x_step, k) for k in range(NZ)]
    steps += [(5.0 + 2.1 * k, x_across, k) for k in range(NZ)]
    for _, step, at in sorted(steps, key=lambda e: e[0]):
        step(at)
        if step is z_step and at == 3:
            go[core, x, z] = g[core, :, x, z, 2]
            for r in NEAR_EIGHT:
                oz_copy(r).start()
    for r in range(1, NZ):
        oz_copy(r).wait_recv()
    for r in (1, 3, 2):
        ox_copy(r).start()
    o_core_copy(0).start()

    def arrived(c):
        own[c].wait()
        for r in range(1, SEQ):
            forth(c, r).wait_recv()

    parts = (slice(0, 6), slice(6, BACK))

    def give_back(c, part, r):
        to = (s_me + r) % SEQ
        return remote(
            back.at[c, to, parts[part]], got.at[c, s_me, parts[part]], r_s.at[c, part, r], r_r.at[c, part, r], seq_id(to)
        )

    def keep(c):
        return pltpu.make_async_copy(back.at[c, s_me], got.at[c, s_me], own_sem.at[c])

    def clip(c):
        for part in range(2):
            attend(c, part, xm, wt, qkv_t, att_t, back, cos_t, even_t, odd_t, mask_t)
            for r in FAR_SEQ:
                give_back(c, part, r).start()
        keep(c).start()

    arrived(0)
    loads[2].wait()
    normalise(xin, xm, mod_ref, 0)
    for k in range(NZ):
        for xr in range(NX):
            core_copy(xr, k).wait_recv()
    unpack_qkv(g, wt)

    clip(0)
    hold.start()
    for r in (1, 3, 2):
        ox_copy(r).wait_recv()
        o_core_copy(NX - r).start()
    arrived(1)
    normalise(xin, xm, mod_ref, 1)
    clip(1)
    for xr in range(NX):
        o_core_copy(xr).wait_recv()
    unpack_out(go, wot)
    hold.wait()
    for r in range(1, NY):
        piece(r).wait_send()
    for c in range(C):
        for r in range(1, SEQ):
            forth(c, r).wait_send()
    for way in range(2):
        for m in range(1, NZ // 2 + 1):
            z_copy(way, m).wait_send()
        for k in range(NZ):
            x_copy(way, k, 1).wait_send()
    for k in range(NZ):
        x_copy(k % 2, k, 2).wait_send()
    for r in range(1, NZ):
        oz_copy(r).wait_send()
    for r in range(1, NX):
        ox_copy(r).wait_send()
    for xr in range(NX):
        o_core_copy(xr).wait_send()
        for k in range(NZ):
            core_copy(xr, k).wait_send()

    def out_copy(c, f):
        return pltpu.make_async_copy(outv.at[c, f], out.at[c, f], out_sem.at[c, f])

    for c in range(C):
        keep(c).wait()
        for part in range(2):
            for r in range(1, SEQ):
                give_back(c, part, r).wait_send()
        for part in range(2):
            for r in range(1, SEQ):
                give_back(c, part, r).wait_recv()
        gate = mod_ref[2, c : c + 1, :]
        for f in range(TL):
            lanes = [got[c, :, at].astype(F32).reshape(SEQ * PL, 128) for at in (f, 3 + f, 6 + f, 9 + f, 12 + f // 2)]
            if f == 1:
                a = jnp.concatenate(lanes[:4], axis=1).astype(BF16)
                p = nn(a, wot[:512]) + nn(lanes[4].astype(BF16), wot[VD + 64 : VD + 192])
            else:
                p = nn(jnp.concatenate(lanes, axis=1).astype(BF16), wot[: VD + 64])
            live = jnp.where(TL * s_me + f < cf_ref[c], 1.0, 0.0)
            res = held[c, f].astype(F32).reshape(SEQ * PL, D) + (live * gate) * p
            outv[c, f] = res.reshape(SEQ, PL, D).astype(BF16)
            out_copy(c, f).start()

    for c in range(C):
        for f in range(TL):
            out_copy(c, f).wait()


def hand_out(src, dst, buf, in_sem, out_sem):
    blocks = [(c, f) for c in range(C) for f in range(TL)]
    into = [pltpu.make_async_copy(src.at[at], buf.at[at], in_sem.at[at]) for at in blocks]
    onto = [pltpu.make_async_copy(buf.at[at], dst.at[at], out_sem.at[at]) for at in blocks]
    for copy in into:
        copy.start()
    for one, other in zip(into, onto):
        one.wait()
        other.start()
    for copy in onto:
        copy.wait()


def shards(latents, modulation, w_qkv, w_out, clip_frames, time_positions):
    smem = pl.BlockSpec(memory_space=pltpu.SMEM)
    hbm = pl.BlockSpec(memory_space=pl.ANY)
    dma = pltpu.SemaphoreType.DMA
    grouped = latents.reshape(C, TL, SEQ, PL, D)
    out = pl.pallas_call(
        kernel,
        out_shape=jax.ShapeDtypeStruct(grouped.shape, BF16),
        in_specs=[hbm, hbm, hbm, hbm, smem, smem],
        out_specs=hbm,
        scratch_shapes=[
            pltpu.VMEM((3, C, D), F32),
            pltpu.VMEM((3 * VD // SEQ, D), BF16),
            pltpu.VMEM((VD // SEQ, D), BF16),
            pltpu.VMEM((C, SEQ, TL, PL, D), BF16),
            pltpu.VMEM((C, TOK, D), BF16),
            pltpu.VMEM((NX, NZ, 3, 16, 128), BF16),
            pltpu.VMEM((2, NY, NX, NZ, 3, 16, 128), BF16),
            pltpu.VMEM((2, NX, NZ, NY, 16, 128), BF16),
            pltpu.VMEM((3 * QK, D), BF16),
            pltpu.VMEM((VD + 192, D), BF16),
            pltpu.VMEM((3 * QK, TOK), BF16),
            pltpu.VMEM((VD, TOK), F32),
            pltpu.VMEM((C, SEQ, BACK, PL, 128), BF16),
            pltpu.VMEM((C, SEQ, BACK, PL, 128), BF16),
            pltpu.VMEM((C, TL, SEQ, PL, D), BF16),
            pltpu.VMEM((C, TL, SEQ, PL, D), BF16),
            pltpu.VMEM((C, HP, TOK), F32),
            pltpu.VMEM((C, HP, TOK), F32),
            pltpu.VMEM((C, HP, TOK), F32),
            pltpu.VMEM((C, TOK, TOK), BF16),
            dma((NY,)), dma((NY,)),
            dma((2, 5)), dma((2, 5)),
            dma((4, NZ)), dma((4, NZ)),
            dma((NX, NZ)), dma((NX, NZ)),
            dma((NZ,)), dma((NZ,)),
            dma((NX,)), dma((NX,)),
            dma((NX,)), dma((NX,)),
            dma((C, SEQ)), dma((C, SEQ)),
            dma((C, 2, SEQ)), dma((C, 2, SEQ)),
            dma((C,)), dma((3,)), dma, dma((C, TL)),
        ],
        compiler_params=pltpu.CompilerParams(
            collective_id=0, has_side_effects=True, vmem_limit_bytes=56 * 1024 * 1024
        ),
        cost_estimate=pl.CostEstimate(flops=6 * 10**9, bytes_accessed=8 * 10**6, transcendentals=10**7),
    )(grouped, modulation.transpose(1, 0, 2), w_qkv.T, w_out, clip_frames, time_positions)
    out = pl.pallas_call(
        hand_out,
        out_shape=jax.ShapeDtypeStruct(grouped.shape, BF16),
        in_specs=[hbm],
        out_specs=hbm,
        scratch_shapes=[pltpu.VMEM(grouped.shape, BF16), dma((C, TL)), dma((C, TL))],
        cost_estimate=pl.CostEstimate(flops=0, bytes_accessed=4 * 10**6, transcendentals=0),
    )(out)
    return out.reshape(latents.shape)


def solution(mesh):
    return jax.shard_map(
        shards,
        mesh=mesh,
        in_specs=(
            P("dp", "seq", None, None),
            P("dp", None, None),
            P(None, "seq"),
            P("seq", None),
            P("dp"),
            P("dp", None),
        ),
        out_specs=P("dp", "seq", None, None),
        check_vma=False,
    )
```

```python
import functools
import math

import jax
import jax.numpy as jnp
from jax import lax
from jax.experimental import pallas as pl
from jax.experimental.pallas import tpu as pltpu
from jax.sharding import PartitionSpec as P

MESH = pl.DeviceIdType.MESH
F32 = jnp.float32
BF16 = jnp.bfloat16

D = 1152
H = 8
HD = 72
C = 2
T = 48
SEQ = 16
NX = 4
NZ = 8
NY = 8
TL = 3
PL = 8
TOK = T * PL
HP = 80
QK = H * HP
VD = H * HD
BACK = 14
KT = D // 128
ZREL = (0, 1, 7, 2, 6, 3, 5, 4)
NEAR_SEQ = (1, 15, 2, 14, 3, 13, 4, 12, 5, 11, 6, 10, 7, 9, 8)
FAR_SEQ = NEAR_SEQ[::-1]
LATE = 5
NEAR_EIGHT = (1, 7, 2, 6, 3, 5, 4)


def nt(a, b):
    return lax.dot_general(a, b, (((1,), (1,)), ((), ())), preferred_element_type=F32)


def nn(a, b):
    return lax.dot_general(a, b, (((1,), (0,)), ((), ())), preferred_element_type=F32)


def row_ids(shape):
    return lax.broadcasted_iota(jnp.int32, shape, 0)


def lane_ids(shape):
    return lax.broadcasted_iota(jnp.int32, shape, 1)


def normalise(xin, xm, mod_ref, c):
    @pl.loop(0, SEQ // 2)
    def _(k):
        v = xin[c, pl.ds(2 * k, 2)].astype(F32).reshape(2 * TL * PL, D)
        mean = jnp.mean(v, axis=-1, keepdims=True)
        v = v - mean
        var = jnp.mean(v * v, axis=-1, keepdims=True)
        normed = v * lax.rsqrt(var + 1e-6)
        shift = mod_ref[0, c : c + 1, :]
        scale = mod_ref[1, c : c + 1, :]
        rows = pl.ds(pl.multiple_of(48 * k, 48), 48)
        xm[c, rows, :] = (normed * (1.0 + scale) + shift).astype(BF16)


def tables(tp_ref, cf_ref, cos_t, even_t, odd_t, mask_t):
    shape = (HP, TOK)
    r = row_ids(shape)
    pair = lax.shift_right_logical(r, 1)
    freq = jnp.exp(pair.astype(F32) * (-math.log(10000.0) * 2.0 / HD))
    is_even = (r & 1) == 0
    frame = lax.shift_right_logical(lane_ids((8, TOK)), 3)
    key = row_ids((TOK, TOK))
    query = lane_ids((TOK, TOK))
    same = (key & 7) == (query & 7)
    key_frame = lax.shift_right_logical(key, 3)
    for c in range(C):
        pos = jnp.zeros((8, TOK), F32)
        for t in range(T):
            pos = jnp.where(frame == t, tp_ref[c, t].astype(F32), pos)
        angle = freq * pos[0:1]
        sine = jnp.sin(angle)
        cos_t[c] = jnp.cos(angle)
        even_t[c] = jnp.where(is_even, -sine, 0.0)
        odd_t[c] = jnp.where(is_even, 0.0, sine)
        live = same & (key_frame < cf_ref[c])
        mask_t[c] = jnp.where(live, 1.0, 0.0).astype(BF16)


def pack_weights(wq_ref, wo_ref, wloc):
    for i in range(64):
        d, j = divmod(i, 2)
        kt, rt = divmod(i, 7)
        if kt < KT and rt < 6:
            tile = wq_ref[16 * rt : 16 * rt + 16, 128 * kt : 128 * kt + 128]
        elif kt < KT:
            part = wq_ref[96:108, 128 * kt : 128 * kt + 128].astype(F32)
            tile = jnp.concatenate([part, jnp.zeros((4, 128), F32)], axis=0).astype(BF16)
        else:
            tile = jnp.zeros((16, 128), BF16)
        wloc[d // NZ, d % NZ, j] = tile
    for d in range(32):
        kt, rt = divmod(d, 3)
        if kt < KT and rt < 2:
            tile = wo_ref[16 * rt : 16 * rt + 16, 128 * kt : 128 * kt + 128]
        elif kt < KT:
            part = wo_ref[32:36, 128 * kt : 128 * kt + 128].astype(F32)
            tile = jnp.concatenate([part, jnp.zeros((12, 128), F32)], axis=0).astype(BF16)
        else:
            tile = jnp.zeros((16, 128), BF16)
        wloc[d // NZ, d % NZ, 2] = tile


def join(first, second, rows):
    second = pltpu.roll(second, 4, 0)
    cut = rows - 4
    return jnp.concatenate([first[:cut], first[cut : cut + 8] + second[:8], second[8 : rows + 4]], axis=0)


def unpack_qkv(g, wt):
    @pl.loop(0, NY)
    def _(y):
        for kt in range(KT):
            shard = []
            for core in range(2):
                tiles = []
                for i in range(7 * kt, 7 * kt + 7):
                    d, j = divmod(i, 2)
                    tiles.append(g[core, y, d // NZ, d % NZ, j].astype(F32))
                shard.append(jnp.concatenate(tiles, axis=0))
            w = join(shard[0], shard[1], 108)
            gap = jnp.zeros((8, 128), F32)
            rows = [w[0:72], gap, w[72:144], gap, w[144:216], gap]
            block = jnp.concatenate(rows, axis=0).astype(BF16)
            wt[pl.ds(pl.multiple_of(240 * y, 240), 240), 128 * kt : 128 * kt + 128] = block


def unpack_out(go, wot):
    @pl.loop(0, NY // 2)
    def _(i):
        for kt in range(KT):
            rows = []
            for j in range(2):
                shard = []
                for core in range(2):
                    tiles = []
                    for d in range(3 * kt, 3 * kt + 3):
                        tiles.append(go[core, d // NZ, d % NZ, 2 * i + j].astype(F32))
                    shard.append(jnp.concatenate(tiles, axis=0))
                rows.append(join(shard[0], shard[1], 36))
            block = jnp.concatenate(rows, axis=0).astype(BF16)
            wot[pl.ds(pl.multiple_of(144 * i, 144), 144), 128 * kt : 128 * kt + 128] = block

    wot[VD : VD + 128] = jnp.zeros((128, D), BF16)
    wot[VD + 128 : VD + 192] = wot[VD - 64 : VD]


def rotate(v, cos, even, odd):
    total = jnp.sum(v * v, axis=0, keepdims=True)
    v = v * lax.rsqrt(total * (1.0 / HD) + 1e-6)
    up = pltpu.roll(v, HP - 1, 0)
    down = pltpu.roll(v, 1, 0)
    return (v * cos + up * even + down * odd).astype(BF16)


def attend(c, part, xm, wt, qkv_t, att_t, back, cos_t, even_t, odd_t, mask_t):
    x = xm[c]
    for block in range(3):
        first = QK * block + QK // 2 * part
        rows = slice(first, first + QK // 2)
        qkv_t[rows, :] = nt(wt[rows, :], x).astype(BF16)

    ones_row = jnp.where(row_ids((HP, 1)) == HD, 1.0, 0.0).astype(BF16)
    for h in range(4 * part, 4 * part + 4):
        rows = HP * h
        cos, even, odd = cos_t[c], even_t[c], odd_t[c]
        q = rotate(qkv_t[rows : rows + HP].astype(F32), cos, even, odd)
        k = rotate(qkv_t[QK + rows : QK + rows + HP].astype(F32), cos, even, odd)
        v = qkv_t[2 * QK + rows : 2 * QK + rows + HP] + ones_row
        s = nn(k.T, q)
        e = jnp.exp(s * (1.0 / math.sqrt(HD))).astype(BF16) * mask_t[c]
        o = nn(v, e)
        att_t[HD * h : HD * h + HD] = o[:HD] / o[HD : HD + 1]
    for j in (2 * part, 2 * part + 1):
        turned = att_t[128 * j : 128 * j + 128].T.reshape(SEQ, TL, PL, 128)
        back[c, :, 3 * j : 3 * j + 3] = turned.astype(BF16)
    if part:
        last = att_t[VD - 64 : VD]
        turned = jnp.concatenate([last, last], axis=0).T.reshape(SEQ, TL, PL, 128)
        lane = lax.broadcasted_iota(jnp.int32, (SEQ, PL, 128), 2)
        back[c, :, 12] = jnp.where(lane < 64, turned[:, 0], turned[:, 1]).astype(BF16)
        back[c, :, 13] = turned[:, 2].astype(BF16)


def kernel(
    lat, mod_in, wq_in, wo_in, cf_ref, tp_ref, out,
    mod_ref, wq_ref, wo_ref, xin, xm, wloc, g, go, wt, wot, qkv_t, att_t, back, got, held, outv, cos_t, even_t, odd_t, mask_t,
    a_s, a_r, z_s, z_r, x_s, x_r, cq_s, cq_r, oz_s, oz_r, ox_s, ox_r, co_s, co_r, f_s, f_r, r_s, r_r, own_sem, in_sem, held_sem, out_sem,
):
    s_me = lax.axis_index("seq")
    d_me = lax.axis_index("dp")
    y, core = s_me // 2, s_me % 2
    z, x = d_me // NX, d_me % NX

    def seq_id(s):
        return (s, d_me)

    def plane_id(zz, xx):
        return (s_me, zz * NX + xx)

    sibling = seq_id(s_me + 1 - 2 * core)

    def remote(src, dst, send, recv, to):
        return pltpu.make_async_remote_copy(
            src_ref=src, dst_ref=dst, send_sem=send, recv_sem=recv, device_id=to, device_id_type=MESH
        )

    barrier = pltpu.get_barrier_semaphore()
    for r in range(1, SEQ):
        pl.semaphore_signal(barrier, inc=1, device_id=seq_id((s_me + r) % SEQ), device_id_type=MESH)
    z_next = (plane_id((z + 1) % NZ, x), plane_id((z + NZ - 1) % NZ, x))
    x_next = (plane_id(z, (x + 1) % NX), plane_id(z, (x + NX - 1) % NX))
    for r in range(1, NZ):
        pl.semaphore_signal(barrier, inc=1, device_id=plane_id((z + r) % NZ, x), device_id_type=MESH)
    for r in range(1, NX):
        pl.semaphore_signal(barrier, inc=1, device_id=plane_id(z, (x + r) % NX), device_id_type=MESH)

    loads = [
        pltpu.make_async_copy(wq_in, wq_ref, in_sem.at[0]),
        pltpu.make_async_copy(wo_in, wo_ref, in_sem.at[1]),
        pltpu.make_async_copy(mod_in, mod_ref, in_sem.at[2]),
    ]
    for copy in loads:
        copy.start()
    own = [pltpu.make_async_copy(lat.at[c, :, s_me], xin.at[c, s_me], own_sem.at[c]) for c in range(C)]
    for c in range(C):
        own[c].start()
    hold = pltpu.make_async_copy(lat, held, held_sem)
    for copy in loads[:2]:
        copy.wait()
    pack_weights(wq_ref, wo_ref, wloc)
    g[core, y, x, z] = wloc[x, z]
    pl.semaphore_wait(barrier, SEQ - 1 + NZ - 1 + NX - 1)

    def piece(r):
        yy = (y + r) % NY
        return remote(wloc.at[x, z], g.at[core, y, x, z], a_s.at[r], a_r.at[r], seq_id(2 * yy + core))

    for r in NEAR_EIGHT:
        piece(r).start()

    def forth(c, r):
        to = (s_me + r) % SEQ
        return remote(lat.at[c, :, to], xin.at[c, s_me], f_s.at[c, r], f_r.at[c, r], seq_id(to))

    for r in NEAR_SEQ:
        forth(0, r).start()

    half = (slice(0, NY // 2), slice(NY // 2, NY))
    tiles = slice(0, 2)

    def z_copy(way, m):
        zz = (z + (NZ - m if way == 0 else m) + 1 - 2 * way) % NZ
        ys = half[way] if m == NZ // 2 else slice(None)
        block = g.at[core, ys, x, zz, tiles]
        return remote(block, block, z_s.at[way, m], z_r.at[way, m], z_next[way])

    def x_copy(way, k, behind):
        xx = (x + (NX - behind if way == 0 else behind) + 1 - 2 * way) % NX
        block = g.at[core, :, xx, (z + ZREL[k]) % NZ, tiles]
        n = 2 * (behind - 1) + way
        return remote(block, block, x_s.at[n, k], x_r.at[n, k], x_next[way])

    def core_copy(xr, k):
        block = g.at[core, :, (x + xr) % NX, (z + ZREL[k]) % NZ, tiles]
        return remote(block, block, cq_s.at[xr, k], cq_r.at[xr, k], sibling)

    def far(k):
        block = g.at[core, :, x, (z + ZREL[k]) % NZ, tiles]
        return remote(block, block, x_s.at[2 + k % 2, k], x_r.at[2 + k % 2, k], plane_id(z, (x + 2) % NX))

    def column(k):
        x_copy(0, k, 1).start()
        x_copy(1, k, 1).start()
        if k >= LATE:
            far(k).start()
        core_copy(0, k).start()

    def z_step(m):
        for way in range(2):
            z_copy(way, m).wait_recv()
            if m < NZ // 2:
                z_copy(way, m + 1).start()
                column(2 * m - way)
        if m == NZ // 2:
            column(7)

    def x_step(k):
        for way in (k % 2, 1 - k % 2):
            x_copy(way, k, 1).wait_recv()
            if way == k % 2 and k < LATE:
                x_copy(way, k, 2).start()
            core_copy((3, 1)[way], k).start()

    def x_across(k):
        x_copy(k % 2, k, 2).wait_recv()
        core_copy(2, k).start()

    def oz_copy(r):
        mine = g.at[core, :, x, z, 2]
        return remote(mine, go.at[core, x, z], oz_s.at[r], oz_r.at[r], plane_id((z + r) % NZ, x))

    def ox_copy(r):
        block = go.at[core, x]
        return remote(block, block, ox_s.at[r], ox_r.at[r], plane_id(z, (x + r) % NX))

    def o_core_copy(xr):
        block = go.at[core, (x + xr) % NX]
        return remote(block, block, co_s.at[xr], co_r.at[xr], sibling)

    for r in NEAR_EIGHT:
        piece(r).wait_recv()
    for way in range(2):
        z_copy(way, 1).start()
    column(0)
    for r in NEAR_SEQ:
        forth(1, r).start()
    tables(tp_ref, cf_ref, cos_t, even_t, odd_t, mask_t)

    steps = [(2.4 * m, z_step, m) for m in range(1, 5)]
    steps += [(2.6 + 2.1 * k, x_step, k) for k in range(NZ)]
    steps += [(5.0 + 2.1 * k, x_across, k) for k in range(NZ)]
    for _, step, at in sorted(steps, key=lambda e: e[0]):
        step(at)
        if step is z_step and at == 3:
            go[core, x, z] = g[core, :, x, z, 2]
            for r in NEAR_EIGHT:
                oz_copy(r).start()
    for r in range(1, NZ):
        oz_copy(r).wait_recv()
    for r in (1, 3, 2):
        ox_copy(r).start()
    o_core_copy(0).start()

    def arrived(c):
        own[c].wait()
        for r in range(1, SEQ):
            forth(c, r).wait_recv()

    parts = (slice(0, 6), slice(6, BACK))

    def give_back(c, part, r):
        to = (s_me + r) % SEQ
        return remote(
            back.at[c, to, parts[part]], got.at[c, s_me, parts[part]], r_s.at[c, part, r], r_r.at[c, part, r], seq_id(to)
        )

    def keep(c):
        return pltpu.make_async_copy(back.at[c, s_me], got.at[c, s_me], own_sem.at[c])

    def clip(c):
        for part in range(2):
            attend(c, part, xm, wt, qkv_t, att_t, back, cos_t, even_t, odd_t, mask_t)
            for r in FAR_SEQ:
                give_back(c, part, r).start()
        keep(c).start()

    arrived(0)
    loads[2].wait()
    normalise(xin, xm, mod_ref, 0)
    for k in range(NZ):
        for xr in range(NX):
            core_copy(xr, k).wait_recv()
    unpack_qkv(g, wt)

    clip(0)
    hold.start()
    for r in (1, 3, 2):
        ox_copy(r).wait_recv()
        o_core_copy(NX - r).start()
    arrived(1)
    normalise(xin, xm, mod_ref, 1)
    clip(1)
    for xr in range(NX):
        o_core_copy(xr).wait_recv()
    unpack_out(go, wot)
    hold.wait()
    for r in range(1, NY):
        piece(r).wait_send()
    for c in range(C):
        for r in range(1, SEQ):
            forth(c, r).wait_send()
    for way in range(2):
        for m in range(1, NZ // 2 + 1):
            z_copy(way, m).wait_send()
        for k in range(NZ):
            x_copy(way, k, 1).wait_send()
    for k in range(NZ):
        x_copy(k % 2, k, 2).wait_send()
    for r in range(1, NZ):
        oz_copy(r).wait_send()
    for r in range(1, NX):
        ox_copy(r).wait_send()
    for xr in range(NX):
        o_core_copy(xr).wait_send()
        for k in range(NZ):
            core_copy(xr, k).wait_send()

    def out_copy(c, f):
        return pltpu.make_async_copy(outv.at[c, f], out.at[c, f], out_sem.at[c, f])

    for c in range(C):
        keep(c).wait()
        for part in range(2):
            for r in range(1, SEQ):
                give_back(c, part, r).wait_send()
        for part in range(2):
            for r in range(1, SEQ):
                give_back(c, part, r).wait_recv()
        gate = mod_ref[2, c : c + 1, :]
        for f in range(TL):
            lanes = [got[c, :, at].astype(F32).reshape(SEQ * PL, 128) for at in (f, 3 + f, 6 + f, 9 + f, 12 + f // 2)]
            if f == 1:
                a = jnp.concatenate(lanes[:4], axis=1).astype(BF16)
                p = nn(a, wot[:512]) + nn(lanes[4].astype(BF16), wot[VD + 64 : VD + 192])
            else:
                p = nn(jnp.concatenate(lanes, axis=1).astype(BF16), wot[: VD + 64])
            live = jnp.where(TL * s_me + f < cf_ref[c], 1.0, 0.0)
            res = held[c, f].astype(F32).reshape(SEQ * PL, D) + (live * gate) * p
            outv[c, f] = res.reshape(SEQ, PL, D).astype(BF16)
            out_copy(c, f).start()

    for c in range(C):
        for f in range(TL):
            out_copy(c, f).wait()


def hand_out(src, dst, buf, in_sem, out_sem):
    blocks = [(c, f) for c in range(C) for f in range(TL)]
    into = [pltpu.make_async_copy(src.at[at], buf.at[at], in_sem.at[at]) for at in blocks]
    onto = [pltpu.make_async_copy(buf.at[at], dst.at[at], out_sem.at[at]) for at in blocks]
    for copy in into:
        copy.start()
    for one, other in zip(into, onto):
        one.wait()
        other.start()
    for copy in onto:
        copy.wait()


def shards(latents, modulation, w_qkv, w_out, clip_frames, time_positions):
    smem = pl.BlockSpec(memory_space=pltpu.SMEM)
    hbm = pl.BlockSpec(memory_space=pl.ANY)
    dma = pltpu.SemaphoreType.DMA
    grouped = latents.reshape(C, TL, SEQ, PL, D)
    out = pl.pallas_call(
        kernel,
        out_shape=jax.ShapeDtypeStruct(grouped.shape, BF16),
        in_specs=[hbm, hbm, hbm, hbm, smem, smem],
        out_specs=hbm,
        scratch_shapes=[
            pltpu.VMEM((3, C, D), F32),
            pltpu.VMEM((3 * VD // SEQ, D), BF16),
            pltpu.VMEM((VD // SEQ, D), BF16),
            pltpu.VMEM((C, SEQ, TL, PL, D), BF16),
            pltpu.VMEM((C, TOK, D), BF16),
            pltpu.VMEM((NX, NZ, 3, 16, 128), BF16),
            pltpu.VMEM((2, NY, NX, NZ, 3, 16, 128), BF16),
            pltpu.VMEM((2, NX, NZ, NY, 16, 128), BF16),
            pltpu.VMEM((3 * QK, D), BF16),
            pltpu.VMEM((VD + 192, D), BF16),
            pltpu.VMEM((3 * QK, TOK), BF16),
            pltpu.VMEM((VD, TOK), F32),
            pltpu.VMEM((C, SEQ, BACK, PL, 128), BF16),
            pltpu.VMEM((C, SEQ, BACK, PL, 128), BF16),
            pltpu.VMEM((C, TL, SEQ, PL, D), BF16),
            pltpu.VMEM((C, TL, SEQ, PL, D), BF16),
            pltpu.VMEM((C, HP, TOK), F32),
            pltpu.VMEM((C, HP, TOK), F32),
            pltpu.VMEM((C, HP, TOK), F32),
            pltpu.VMEM((C, TOK, TOK), BF16),
            dma((NY,)), dma((NY,)),
            dma((2, 5)), dma((2, 5)),
            dma((4, NZ)), dma((4, NZ)),
            dma((NX, NZ)), dma((NX, NZ)),
            dma((NZ,)), dma((NZ,)),
            dma((NX,)), dma((NX,)),
            dma((NX,)), dma((NX,)),
            dma((C, SEQ)), dma((C, SEQ)),
            dma((C, 2, SEQ)), dma((C, 2, SEQ)),
            dma((C,)), dma((3,)), dma, dma((C, TL)),
        ],
        compiler_params=pltpu.CompilerParams(
            collective_id=0, has_side_effects=True, vmem_limit_bytes=56 * 1024 * 1024
        ),
        cost_estimate=pl.CostEstimate(flops=6 * 10**9, bytes_accessed=8 * 10**6, transcendentals=10**7),
    )(grouped, modulation.transpose(1, 0, 2), w_qkv.T, w_out, clip_frames, time_positions)
    out = pl.pallas_call(
        hand_out,
        out_shape=jax.ShapeDtypeStruct(grouped.shape, BF16),
        in_specs=[hbm],
        out_specs=hbm,
        scratch_shapes=[pltpu.VMEM(grouped.shape, BF16), dma((C, TL)), dma((C, TL))],
        cost_estimate=pl.CostEstimate(flops=0, bytes_accessed=4 * 10**6, transcendentals=0),
    )(out)
    return out.reshape(latents.shape)


def solution(mesh):
    return jax.shard_map(
        shards,
        mesh=mesh,
        in_specs=(
            P("dp", "seq", None, None),
            P("dp", None, None),
            P(None, "seq"),
            P("seq", None),
            P("dp"),
            P("dp", None),
        ),
        out_specs=P("dp", "seq", None, None),
        check_vma=False,
    )
```
